256 devices in a mesh: row: 16 (over y, x), col: 16 (over z, core).
Axes of the slice: x: 4, y: 4, z: 8, core: 2. Of those that a mesh axis runs over, the one named last changes fastest.
Arguments:
- x_panels: bfloat16 [2, 16, 96, 128, 128], P(None, 'row', 'col'), may hold values from -0.5 to 0.5
- square_panels: bfloat16 [2, 16, 192, 128, 128], P(None, 'row', 'col'), may hold values from -6 to 6
- x_blocks: bfloat16 [16, 512, 128, 128], P('row', 'col'), may hold values from -6 to 6
- pair_lists: int32 [16, 16, 2, 3, 128], P('row', 'col'), may hold values from 0 to 191, as said below
- pair_counts: int32 [16, 16, 2], P('row', 'col'), may hold values from 16 to 128, as said below
Outputs:
- new_blocks: bfloat16 [16, 512, 128, 128], P('row', 'col')
The draws below stay inside these ranges and needn't reach their ends.
Inputs may be any that keep to these rules, and one draw needn't show every extreme that they name: `pair_lists`: entry 0 of every index list is 0 and the largest index is reached at every device. For e < 16 the first index lies in [e * 6, (e + 1) * 6), for e < 16 the second in [e * 12, (e + 1) * 12). `pair_counts`: in each panel some device has a full list.
All inputs are finite; a program needn't handle non-finite values.
Results may differ from the reference program's by a relative error of at most 0.001.
Values may be sent and summed in bfloat16 or wider, within the bound.
No kernel may reach another device: no remote copies, remote signals or barrier semaphores. Data moves between devices by JAX's collectives and lax.ppermute only.
A program may use at most 128 MiB of HBM per device.

```python
import jax
import jax.numpy as jnp
from jax import lax

BS = 128
ASLOT = 6
BSLOT = 12
OSLOT = 32
PAIRS = 128
N_ROW = 16
N_COL = 16


def draw_pair_lists(key, part):
    key = jax.random.fold_in(key, 11)
    keys = jax.random.split(key, 5)
    shape = (N_ROW, N_COL, 2, PAIRS)
    position = jnp.arange(PAIRS, dtype=jnp.int32)
    first = jax.random.randint(keys[0], shape, 0, N_COL * ASLOT, dtype=jnp.int32)
    first_cover = position * ASLOT + jax.random.randint(keys[1], shape, 0, ASLOT, dtype=jnp.int32)
    first = jnp.where(position < N_COL, first_cover, first)
    first = first.at[..., 0].set(0)
    first = first.at[..., N_COL - 1].set(N_COL * ASLOT - 1)
    second = jax.random.randint(keys[2], shape, 0, N_ROW * BSLOT, dtype=jnp.int32)
    second_cover = position * BSLOT + jax.random.randint(keys[3], shape, 0, BSLOT, dtype=jnp.int32)
    second = jnp.where(position < N_ROW, second_cover, second)
    second = second.at[..., 0].set(0)
    second = second.at[..., N_ROW - 1].set(N_ROW * BSLOT - 1)
    target = jax.random.randint(keys[4], shape, 0, OSLOT, dtype=jnp.int32)
    target = target.at[..., 0].set(0)
    target = target.at[..., 1].set(OSLOT - 1)
    return jnp.stack([first, second, target], axis=3)


def draw_pair_counts(key, part):
    key = jax.random.fold_in(key, 12)
    keys = jax.random.split(key, 2)
    expon = jax.random.randint(keys[0], (N_ROW * N_COL, 2), 0, 4, dtype=jnp.int32)
    counts = jnp.right_shift(jnp.full((N_ROW * N_COL, 2), PAIRS, jnp.int32), expon)
    busiest = jax.random.randint(keys[1], (2,), 0, N_ROW * N_COL, dtype=jnp.int32)
    counts = counts.at[busiest, jnp.arange(2, dtype=jnp.int32)].set(PAIRS)
    return counts.reshape(N_ROW, N_COL, 2)


def block_levels(key, shape, cuts, least, largest):
    factor_of, own = 1.0, jax.random.fold_in(key, 6)
    for dim, shards_of in cuts:
        draws = jnp.exp(jax.random.uniform(jax.random.fold_in(own, dim), (shards_of,), jnp.float32, least / len(cuts), largest / len(cuts)))
        factor_of = factor_of * jnp.repeat(draws, shape[dim] // shards_of).reshape([-1 if axis == dim else 1 for axis in range(len(shape))])
    return factor_of


def normal_values(key, shape, scale, limit, shards=(), held_as=jnp.bfloat16):
    factor_of = block_levels(key, shape, shards, -0.22, 0.18) if shards else 1.0
    array = jax.random.normal(key, shape, jnp.float32) * scale * factor_of
    return jnp.minimum(jnp.maximum(array, -limit), limit).astype(held_as)


def setup_inputs(seed: int = 0) -> dict:
    streams_of = jax.random.split(jax.random.key(seed), 6)
    x_panels = normal_values(streams_of[0], (2, N_ROW, N_COL * ASLOT, BS, BS), BS ** -0.5, 0.5, ((1, 16), (2, 16)))
    square_panels = normal_values(streams_of[1], (2, N_ROW, N_COL * BSLOT, BS, BS), 1.0, 6.0, ((1, 16), (2, 16)))
    x_blocks = normal_values(streams_of[2], (N_ROW, N_COL * OSLOT, BS, BS), 1.0, 6.0, ((0, 16), (1, 16)))
    pair_lists = draw_pair_lists(jax.random.fold_in(streams_of[5], 71), 0)
    pair_counts = draw_pair_counts(jax.random.fold_in(streams_of[5], 71), 0)
    return dict(x_panels=x_panels, square_panels=square_panels, x_blocks=x_blocks, pair_lists=pair_lists, pair_counts=pair_counts)


def reference(x_panels, square_panels, x_blocks, pair_lists, pair_counts):
    def one_device(index):
        rowpos = index // N_COL
        colpos = index % N_COL
        total = jnp.zeros((OSLOT, BS, BS), jnp.float32)
        for panel in range(2):
            left = x_panels[panel][rowpos]
            right = lax.dynamic_slice_in_dim(square_panels[panel], (colpos * BSLOT).astype(jnp.int32), BSLOT, 1)
            right = right.reshape(N_ROW * BSLOT, BS, BS)
            lists = pair_lists[rowpos, colpos, panel]
            count = pair_counts[rowpos, colpos, panel]
            first = jnp.take(left, lists[0], axis=0).astype(jnp.float32)
            second = jnp.take(right, lists[1], axis=0).astype(jnp.float32)
            product = jnp.einsum("eij,ejk->eik", first, second, precision=lax.Precision.HIGHEST)
            keep = (jnp.arange(PAIRS, dtype=jnp.int32) < count).astype(jnp.float32)
            total = total.at[lists[2]].add(product * keep[:, None, None])
        own = lax.dynamic_slice_in_dim(x_blocks[rowpos], (colpos * OSLOT).astype(jnp.int32), OSLOT, 0)
        return ((3.0 * own.astype(jnp.float32) - total) * 0.5).astype(jnp.bfloat16)

    result = lax.map(one_device, jnp.arange(N_ROW * N_COL, dtype=jnp.int32))
    return result.reshape(N_ROW, N_COL * OSLOT, BS, BS)
```

```python
import functools

import jax
import jax.numpy as jnp
import numpy as np
from jax import lax
from jax.experimental import pallas as pl
from jax.experimental.pallas import tpu as pltpu
from jax.sharding import PartitionSpec as P

SIDE = 4
GROUP = 16
STAGES = 3


def place_table(shard):
    half = shard // 2
    table = np.zeros((2, SIDE, SIDE, shard), np.int32)
    for panel in range(2):
        for dx in range(SIDE):
            for dy in range(SIDE):
                for j in range(shard):
                    full, part = panel * shard + j, panel * half + j % half
                    near, far = (dx, dy) if panel == 0 else (dy, dx)
                    if dx == 0 and dy == 0:
                        stage, place = 0, full
                    elif dx == 0 or dy == 0:
                        along, base = (dx, 1) if dy == 0 else (dy, 3)
                        if along == 2:
                            order = (0 if dy == 0 else 2) + j // half
                            stage, place = 0, 10 * shard + order * shard + part
                        else:
                            stage, place = 0, 2 * shard * (base + (along == 1)) + full
                    else:
                        q = {3: 0, 1: 1, 2: 2}[near] * shard + j
                        if far == 2:
                            stage, place = 2, 3 * shard * panel + q
                        else:
                            stage, place = 1, 3 * shard * (2 * panel + (far == 1)) + q
                    table[panel, dx, dy, j] = stage << 12 | place
    return table.reshape(-1)


def sort_kernel(left_shard, right_shard, slots, here, table, lists, counts, entries, groups, lengths):
    x, y = here[0], here[1]
    pairs = lists.shape[-1]
    for stage in range(STAGES):
        lengths[stage] = 0
    for panel in range(2):

        def add(e, carry, panel=panel):
            first = lists[panel * 3, e]
            second = lists[panel * 3 + 1, e]
            slot = lists[panel * 3 + 2, e]
            left_owner = (first * (2**16 // left_shard + 1)) >> 16
            left = first + (left_owner + panel) * left_shard
            owner = (second * (2**16 // right_shard + 1)) >> 16
            j = second - owner * right_shard
            dx = ((owner & (SIDE - 1)) - x) & (SIDE - 1)
            dy = ((owner // SIDE) - y) & (SIDE - 1)
            found = table[((panel * SIDE + dx) * SIDE + dy) * right_shard + j]
            stage, place = found >> 12, found & 4095
            at = lengths[stage]
            entries[stage, at] = left | place << 8 | slot << 16
            lengths[stage] = at + 1
            return carry

        lax.fori_loop(0, counts[panel], add, 0)
    for stage in range(STAGES):
        length = lengths[stage]
        for e in range(GROUP - 1):
            entries[stage, length + e] = slots << 16
        groups[stage] = (length + GROUP - 1) // GROUP


def sort_lists(here, table, lists, counts, left_shard, right_shard, slots):
    smem = pl.BlockSpec(memory_space=pltpu.SMEM)
    pairs = lists.shape[-1]
    return pl.pallas_call(
        functools.partial(sort_kernel, left_shard, right_shard, slots),
        out_shape=(
            jax.ShapeDtypeStruct((STAGES, 2 * pairs + GROUP), jnp.int32),
            jax.ShapeDtypeStruct((STAGES,), jnp.int32),
        ),
        in_specs=[smem] * 4,
        out_specs=(smem, smem),
        scratch_shapes=[pltpu.SMEM((STAGES,), jnp.int32)],
        cost_estimate=pl.CostEstimate(flops=0, bytes_accessed=8 * 2**20, transcendentals=0),
        name="sort_lists",
    )(here, table, lists, counts)


def products_kernel(stage, groups, entries, left, right, start, out, *scratch):
    slots = out.shape[0]
    acc = scratch[0] if scratch else out
    if stage == 0:
        count = start.shape[0]
        acc[:count] = -3.0 * start[...].astype(jnp.float32)
        acc[count] = jnp.zeros_like(acc[count])
    else:
        acc[...] = start[...]

    def step(g, carry):
        words = [entries[stage, g * GROUP + e] for e in range(GROUP)]
        made = [
            jnp.dot(left[w & 255], right[(w >> 8) & 255], preferred_element_type=jnp.float32)
            for w in words
        ]
        for w, product in zip(words, made):
            slot = w >> 16
            acc[slot] = acc[slot] + product
        return carry

    lax.fori_loop(0, groups[stage], step, 0)
    if scratch:
        out[...] = (-0.5 * acc[:slots]).astype(out.dtype)


def add_products(stage, groups, entries, left, right, start):
    smem = pl.BlockSpec(memory_space=pltpu.SMEM)
    vmem = pl.BlockSpec(memory_space=pltpu.VMEM)
    block = left.shape[-1]
    last = stage == STAGES - 1
    slots = start.shape[0] + (1 if stage == 0 else -1 if last else 0)
    scratch = [pltpu.VMEM(start.shape, jnp.float32)] if last else []
    return pl.pallas_call(
        functools.partial(products_kernel, stage),
        out_shape=jax.ShapeDtypeStruct((slots, block, block), jnp.bfloat16 if last else jnp.float32),
        in_specs=[smem, smem, vmem, vmem, vmem],
        out_specs=vmem,
        scratch_shapes=scratch,
        cost_estimate=pl.CostEstimate(
            flops=2 * 64 * block**3, bytes_accessed=16 * 2**20, transcendentals=0
        ),
        compiler_params=pltpu.CompilerParams(vmem_limit_bytes=8 * 2**20),
        name="products",
    )(groups, entries, left, right, start)


def shift(blocks, axis, by):
    pairs = []
    for y in range(SIDE):
        for x in range(SIDE):
            to = (y, (x + by) % SIDE) if axis == "x" else ((y + by) % SIDE, x)
            pairs.append((y * SIDE + x, to[0] * SIDE + to[1]))
    return lax.ppermute(blocks, "row", pairs)


def on_device(x_panels, square_panels, x_blocks, pair_lists, pair_counts):
    block = x_blocks.shape[-1]
    left_shard, shard = x_panels.shape[2], square_panels.shape[2]
    half = shard // 2
    left = lax.all_gather(
        x_panels.reshape(2 * left_shard, block, block), "col", axis=0, tiled=True
    )
    row = lax.axis_index("row")
    here = jnp.stack([row % SIDE, row // SIDE]).astype(jnp.int32)
    entries, groups = sort_lists(
        here,
        jnp.asarray(place_table(shard)),
        pair_lists.reshape(6, -1),
        pair_counts.reshape(2),
        left_shard,
        shard,
        x_blocks.shape[1],
    )

    def halves(blocks, which):
        at = which * half
        return jnp.concatenate([blocks[at : at + half], blocks[shard + at : shard + at + half]])

    def products(stage, pieces, start):
        right = pltpu.with_memory_space_constraint(jnp.concatenate(pieces), pltpu.VMEM)
        return add_products(stage, groups, entries, left, right, start)

    own = square_panels.reshape(2 * shard, block, block)
    near = [shift(own, "x", 1), shift(own, "x", -1), shift(own, "y", 1), shift(own, "y", -1)]
    near, entries, groups = lax.optimization_barrier((near, entries, groups))
    right, leftward, up, down = near
    second = [
        shift(halves(right, 0), "x", 1),
        shift(halves(leftward, 1), "x", -1),
        shift(halves(up, 0), "y", 1),
        shift(halves(down, 1), "y", -1),
    ]
    right2, left2, up2, down2 = second
    line_x = jnp.concatenate([right[:shard], leftward[:shard], right2[:half], left2[:half]])
    line_y = jnp.concatenate([up[shard:], down[shard:], up2[half:], down2[half:]])
    far = [shift(line_x, "y", 1), shift(line_x, "y", -1), shift(line_y, "x", 1), shift(line_y, "x", -1)]
    total = products(0, [own] + near + second, x_blocks[0])
    far, total = lax.optimization_barrier((far, total))
    cut = 3 * half
    last = [
        shift(far[0][:cut], "y", 1),
        shift(far[1][cut:], "y", -1),
        shift(far[2][:cut], "x", 1),
        shift(far[3][cut:], "x", -1),
    ]
    total = products(1, far, total)
    return products(2, last, total)[None]


def solution(mesh):
    in_specs = (
        P(None, "row", "col", None, None),
        P(None, "row", "col", None, None),
        P("row", "col", None, None),
        P("row", "col", None, None, None),
        P("row", "col", None),
    )
    out_specs = P("row", "col", None, None)
    return jax.shard_map(
        on_device, mesh=mesh, in_specs=in_specs, out_specs=out_specs, check_vma=False
    )
```

```python
import functools

import jax
import jax.numpy as jnp
import numpy as np
from jax import lax
from jax.experimental import pallas as pl
from jax.experimental.pallas import tpu as pltpu
from jax.sharding import PartitionSpec as P

SIDE = 4
GROUP = 16
STAGES = 3
PARTS = (11, 11, 10)

UNITS = {
    (0, 0): ((0, 0), (0, 1)),
    (3, 0): ((0, 2), (0, 3)),
    (1, 0): ((0, 4), (0, 5)),
    (2, 0): ((0, 6), (0, 7)),
    (0, 3): ((0, 8), (0, 9)),
    (0, 1): ((0, 10), (0, 11)),
    (3, 3): ((0, 12), (0, 13)),
    (1, 1): ((0, 14), (0, 15)),
    (2, 3): ((1, 0), (1, 1)),
    (2, 1): ((1, 2), (1, 3)),
    (3, 2): ((2, 0), (1, 4)),
    (1, 3): ((2, 1), (1, 5)),
    (1, 2): ((2, 2), (1, 6)),
    (3, 1): ((2, 3), (1, 7)),
    (0, 2): ((1, 8), (1, 10)),
    (2, 2): ((1, 9), (1, 11)),
}


def place_right(shard):
    right = np.zeros((2, 2, SIDE, SIDE), np.int32)
    for core in range(2):
        for column in range(2):
            for dx in range(SIDE):
                for dy in range(SIDE):
                    stage, slot = UNITS[(dx, dy) if core == 0 else (dy, dx)][column]
                    right[core, column, dx, dy] = stage << 12 | slot * shard
    return right.reshape(-1)


def sort_kernel(left_shard, shard, depth, pairs, slots, here, right_at, own, got, entries, groups, lengths):
    x, y, z, core = here[0], here[1], here[2], here[3]
    way = 2 * core - 1
    for stage in range(STAGES):
        lengths[stage] = 0
    for column, lists in enumerate((own, got)):
        base = core * 3 * pairs

        def add(e, carry, column=column, lists=lists, base=base):
            first = lists[base + e]
            second = lists[base + pairs + e]
            slot = lists[base + 2 * pairs + e] + column * slots
            owner = (first * (2**16 // left_shard + 1)) >> 16
            steps = (((owner >> 1) - z) * way) & (depth - 1)
            left = first + (2 * steps + ((owner & 1) ^ core) - owner) * left_shard
            owner = (second * (2**16 // shard + 1)) >> 16
            dx = (owner - x) & (SIDE - 1)
            dy = ((owner >> 2) - y) & (SIDE - 1)
            found = right_at[((core * 2 + column) * SIDE + dx) * SIDE + dy]
            stage = found >> 12
            place = (found & 4095) + second - owner * shard
            at = lengths[stage]
            entries[stage, at] = left | place << 8 | slot << 16
            lengths[stage] = at + 1
            return carry

        lax.fori_loop(0, lists[6 * pairs + core], add, 0)
    for stage in range(STAGES):
        length = lengths[stage]
        unused = (2 * slots if stage < 2 else slots) << 16
        for e in range(GROUP - 1):
            entries[stage, length + e] = unused
        groups[stage] = (length + GROUP - 1) // GROUP


def sort_lists(here, own, got, left_shard, shard, depth, pairs, slots):
    smem = pl.BlockSpec(memory_space=pltpu.SMEM)
    return pl.pallas_call(
        functools.partial(sort_kernel, left_shard, shard, depth, pairs, slots),
        out_shape=(
            jax.ShapeDtypeStruct((STAGES, 2 * pairs + GROUP), jnp.int32),
            jax.ShapeDtypeStruct((STAGES,), jnp.int32),
        ),
        in_specs=[smem] * 4,
        out_specs=(smem, smem),
        scratch_shapes=[pltpu.SMEM((STAGES,), jnp.int32)],
        cost_estimate=pl.CostEstimate(flops=0, bytes_accessed=8 * 2**20, transcendentals=0),
        name="sort_lists",
    )(here, jnp.asarray(place_right(shard)), own, got)


def select_kernel(core, own, got, own_left, got_left, unit, pair, sems):
    c = core[0]
    shard, left_shard = own.shape[1], own_left.shape[1]
    copies = [
        pltpu.make_async_copy(own.at[c], unit.at[pl.ds(0, shard)], sems.at[0]),
        pltpu.make_async_copy(got.at[c], unit.at[pl.ds(shard, shard)], sems.at[1]),
        pltpu.make_async_copy(own_left.at[c], pair.at[pl.ds(0, left_shard)], sems.at[2]),
        pltpu.make_async_copy(got_left.at[c], pair.at[pl.ds(left_shard, left_shard)], sems.at[3]),
    ]
    for copy in copies:
        copy.start()
    for copy in copies:
        copy.wait()


def select_panel(core, own, got, own_left, got_left):
    hbm = pl.BlockSpec(memory_space=pl.ANY)
    vmem = pl.BlockSpec(memory_space=pltpu.VMEM)
    block = own.shape[-2:]
    return pl.pallas_call(
        select_kernel,
        out_shape=(
            jax.ShapeDtypeStruct((2 * own.shape[1], *block), own.dtype),
            jax.ShapeDtypeStruct((2 * own_left.shape[1], *block), own.dtype),
        ),
        in_specs=[pl.BlockSpec(memory_space=pltpu.SMEM)] + [hbm] * 4,
        out_specs=(vmem, vmem),
        scratch_shapes=[pltpu.SemaphoreType.DMA((4,))],
        cost_estimate=pl.CostEstimate(flops=0, bytes_accessed=2**20, transcendentals=0),
        name="select_panel",
    )(core.reshape(1), own, got, own_left, got_left)


def products_kernel(stage, groups, entries, left, right, *refs):
    if stage == 0:
        start, acc = refs
        count = start.shape[0]
        acc[:count] = -3.0 * start[...].astype(jnp.float32)
        acc[count:] = jnp.zeros((acc.shape[0] - count, *acc.shape[1:]), jnp.float32)
    elif stage == 1:
        start, acc = refs[0], refs[-1]
        acc[...] = start[...]
    else:
        start, acc, out = refs[0], refs[-1], refs[-2]
        count = start.shape[0]
        at = 0
        for part in refs[1:-2]:
            size = part.shape[0]
            acc[at : at + size] = start[at : at + size] + part[...]
            at += size
        acc[count] = jnp.zeros_like(acc[count])

    def step(g, carry):
        words = [entries[stage, g * GROUP + e] for e in range(GROUP)]
        made = [
            jnp.dot(left[w & 255], right[(w >> 8) & 255], preferred_element_type=jnp.float32)
            for w in words
        ]
        for w, product in zip(words, made):
            slot = w >> 16
            acc[slot] = acc[slot] + product
        return carry

    lax.fori_loop(0, groups[stage], step, 0)
    if stage == 1:
        own = refs[1]
        at = own.shape[0]
        own[...] = acc[:at]
        for part in refs[2:-1]:
            part[...] = acc[at : at + part.shape[0]]
            at += part.shape[0]
    elif stage == 2:
        out[...] = (-0.5 * acc[:count]).astype(out.dtype)


def add_products(stage, groups, entries, left, right, starts, slots):
    smem = pl.BlockSpec(memory_space=pltpu.SMEM)
    vmem = pl.BlockSpec(memory_space=pltpu.VMEM)
    block = left.shape[-1]

    def result(count, dtype=jnp.float32):
        return jax.ShapeDtypeStruct((count, block, block), dtype)

    if stage == 0:
        outs, scratch = [result(2 * slots + 1)], []
    elif stage == 1:
        outs = [result(slots)] + [result(part) for part in PARTS]
        scratch = [pltpu.VMEM((2 * slots + 1, block, block), jnp.float32)]
    else:
        outs = [result(slots, jnp.bfloat16)]
        scratch = [pltpu.VMEM((slots + 1, block, block), jnp.float32)]
    return pl.pallas_call(
        functools.partial(products_kernel, stage),
        out_shape=outs,
        in_specs=[smem, smem] + [vmem] * (2 + len(starts)),
        out_specs=[vmem] * len(outs),
        scratch_shapes=scratch,
        cost_estimate=pl.CostEstimate(flops=2**20, bytes_accessed=2**20, transcendentals=0),
        compiler_params=pltpu.CompilerParams(vmem_limit_bytes=28 * 2**20),
        name="products",
    )(groups, entries, left, right, *starts)


def move(blocks, step):
    depth = lax.axis_size("col") // 2
    pairs = []
    for y in range(SIDE):
        for x in range(SIDE):
            for z in range(depth):
                for core in range(2):
                    tx, ty, tz, tcore = step(x, y, z, core)
                    to = ((ty % SIDE * SIDE + tx % SIDE) * depth + tz % depth) * 2 + tcore
                    pairs.append((((y * SIDE + x) * depth + z) * 2 + core, to))
    return lax.ppermute(blocks, ("row", "col"), pairs)


def sibling(blocks):
    return move(blocks, lambda x, y, z, c: (x, y, z, 1 - c))


def onward(blocks):
    return move(blocks, lambda x, y, z, c: (x, y, z + 1 - 2 * c, c))


def first(forth, back):
    return [
        move(v, lambda x, y, z, c: (x, y + by, z, c) if c else (x + by, y, z, c))
        for v, by in ((forth, 1), (back, -1))
    ]


def second(forth, back):
    return [
        move(v, lambda x, y, z, c: (x + by, y, z, c) if c else (x, y + by, z, c))
        for v, by in ((forth, 1), (back, -1))
    ]


def join(*pieces):
    return jnp.concatenate(pieces)


def on_device(x_panels, square_panels, x_blocks, pair_lists, pair_counts):
    block = x_blocks.shape[-1]
    left_shard, shard = x_panels.shape[2], square_panels.shape[2]
    pairs, slots = pair_lists.shape[-1], x_blocks.shape[1]
    depth = lax.axis_size("col") // 2
    row, col = lax.axis_index("row"), lax.axis_index("col")
    core = (col % 2).astype(jnp.int32)
    here = jnp.stack([row % SIDE, row // SIDE, col // 2, core]).astype(jnp.int32)
    order = lax.optimization_barrier
    scope = jax.named_scope

    own, own_left = square_panels[:, 0], x_panels[:, 0]
    with scope("w0"):
        got = sibling(own)
    with scope("w1"):
        got_left = sibling(own_left)
    lists = join(pair_lists.reshape(-1), pair_counts.reshape(-1))
    with scope("w2"):
        got_lists = sibling(lists)
    unit, pair = select_panel(core, own, got, own_left, got_left)

    with scope("s1"):
        r1, l1 = first(unit, unit)
    with scope("t"):
        t = second(unit, unit)
    entries, groups = sort_lists(here, lists, got_lists, left_shard, shard, depth, pairs, slots)
    passed = [pair]
    for step in range(1, depth):
        with scope(f"z{step}"):
            passed.append(onward(passed[-1]))
    left = join(*passed)
    with scope("s2"):
        s2 = first(r1[:shard], l1[shard:])
    t, ar, al = order((t, r1, l1))
    with scope("a1"):
        a1 = second(ar, al)
    x2 = join(*s2)
    with scope("b"):
        b = second(x2, x2)
    with scope("ga"):
        ga = second(join(a1[0][shard:], l1[shard:]), join(a1[1][shard:], r1[shard:]))
    with scope("gh"):
        gh = second(join(t[0][:shard], b[0][:shard]), join(t[1][shard:], b[1][shard:]))
    near = join(unit, r1, l1, *s2, *t, *a1)
    (total,) = add_products(0, groups, entries, left, near, [x_blocks[0]], slots)
    ga, ar, al, a1 = order((ga, r1, l1, a1))
    with scope("a2"):
        a2 = second(join(a1[0][:shard], al[:shard]), join(a1[1][:shard], ar[:shard]))
    far = join(*b, *ga, *gh)
    total, *theirs = add_products(1, groups, entries, left, far, [total], slots)
    with scope("w3"):
        mine = [sibling(part) for part in theirs]
    return add_products(2, groups, entries, left, join(*a2), [total, *mine], slots)[0][None]


def solution(mesh):
    in_specs = (
        P(None, "row", "col", None, None),
        P(None, "row", "col", None, None),
        P("row", "col", None, None),
        P("row", "col", None, None, None),
        P("row", "col", None),
    )
    out_specs = P("row", "col", None, None)
    return jax.shard_map(
        on_device, mesh=mesh, in_specs=in_specs, out_specs=out_specs, check_vma=False
    )
```

```python
import functools

import jax
import jax.numpy as jnp
import numpy as np
from jax import lax
from jax.experimental import pallas as pl
from jax.experimental.pallas import tpu as pltpu
from jax.sharding import PartitionSpec as P

SIDE = 4
GROUP = 16
STAGES = 3
PARTS = (11, 11, 10)

UNITS = {
    (0, 0): ((0, 0), (0, 1)),
    (3, 0): ((0, 2), (0, 3)),
    (1, 0): ((0, 4), (0, 5)),
    (2, 0): ((0, 6), (0, 7)),
    (0, 3): ((0, 8), (0, 9)),
    (0, 1): ((0, 10), (0, 11)),
    (3, 3): ((0, 12), (0, 13)),
    (1, 1): ((0, 14), (0, 15)),
    (2, 3): ((1, 0), (1, 1)),
    (2, 1): ((1, 2), (1, 3)),
    (3, 2): ((2, 0), (1, 4)),
    (1, 3): ((2, 1), (1, 5)),
    (1, 2): ((2, 2), (1, 6)),
    (3, 1): ((2, 3), (1, 7)),
    (0, 2): ((1, 8), (1, 10)),
    (2, 2): ((1, 9), (1, 11)),
}


def place_right(shard):
    right = np.zeros((2, 2, SIDE, SIDE), np.int32)
    for core in range(2):
        for column in range(2):
            for dx in range(SIDE):
                for dy in range(SIDE):
                    stage, slot = UNITS[(dx, dy) if core == 0 else (dy, dx)][column]
                    right[core, column, dx, dy] = stage << 16 | slot * shard << 8
    return right.reshape(-1)


def sort_kernel(left_shard, shard, depth, pairs, slots, here, right_at, own, got, entries, groups, lengths, left_of, right_of):
    x, y, z, core = here[0], here[1], here[2], here[3]
    way = 2 * core - 1
    for stage in range(STAGES):
        lengths[stage] = 0

    def place(owner, carry):
        steps = (((owner >> 1) - z) * way) & (depth - 1)
        other = (owner & 1) ^ core
        far = depth + 2 + 2 * (depth - 1 - steps) + 1 - other
        at = jnp.where(steps <= depth // 2, 2 * steps + other, far)
        left_of[owner] = (at - owner) * left_shard
        dx = (owner - x) & (SIDE - 1)
        dy = ((owner >> 2) - y) & (SIDE - 1)
        for column in range(2):
            found = right_at[((core * 2 + column) * SIDE + dx) * SIDE + dy]
            right_of[column, owner] = found - (owner * shard << 8)
        return carry

    lax.fori_loop(0, SIDE * SIDE, place, 0)
    base = core * 3 * pairs
    for column, lists in enumerate((own, got)):

        def add(e, carry, column=column, lists=lists):
            first = lists[base + e]
            second = lists[base + pairs + e]
            slot = lists[base + 2 * pairs + e] + column * slots
            left = first + left_of[(first * (2**16 // left_shard + 1)) >> 16]
            found = right_of[column, (second * (2**16 // shard + 1)) >> 16] + (second << 8)
            stage = found >> 16
            at = lengths[stage]
            entries[stage, at] = left | (found & 0xFF00) | slot << 16
            lengths[stage] = at + 1
            return carry

        lax.fori_loop(0, lists[6 * pairs + core], add, 0)
    for stage in range(STAGES):
        length = lengths[stage]
        unused = (2 * slots if stage < 2 else slots) << 16
        for e in range(GROUP - 1):
            entries[stage, length + e] = unused
        groups[stage] = (length + GROUP - 1) // GROUP


def sort_lists(here, own, got, left_shard, shard, depth, pairs, slots):
    smem = pl.BlockSpec(memory_space=pltpu.SMEM)
    return pl.pallas_call(
        functools.partial(sort_kernel, left_shard, shard, depth, pairs, slots),
        out_shape=(
            jax.ShapeDtypeStruct((STAGES, 2 * pairs + GROUP), jnp.int32),
            jax.ShapeDtypeStruct((STAGES,), jnp.int32),
        ),
        in_specs=[smem] * 4,
        out_specs=(smem, smem),
        scratch_shapes=[
            pltpu.SMEM((STAGES,), jnp.int32),
            pltpu.SMEM((SIDE * SIDE,), jnp.int32),
            pltpu.SMEM((2, SIDE * SIDE), jnp.int32),
        ],
        cost_estimate=pl.CostEstimate(flops=0, bytes_accessed=8 * 2**20, transcendentals=0),
        name="sort_lists",
    )(here, jnp.asarray(place_right(shard)), own, got)


def select_kernel(core, own, own_left, keep, give, left, sems):
    c = core[0]
    size = own_left.shape[1]
    copies = [
        pltpu.make_async_copy(own.at[1 - c], give, sems.at[0]),
        pltpu.make_async_copy(own.at[c], keep, sems.at[1]),
        pltpu.make_async_copy(own_left.at[c], left.at[pl.ds(0, size)], sems.at[2]),
        pltpu.make_async_copy(own_left.at[1 - c], left.at[pl.ds(size, size)], sems.at[3]),
    ]
    for copy in copies:
        copy.start()
    for copy in copies:
        copy.wait()


def select_panels(core, own, own_left):
    hbm = pl.BlockSpec(memory_space=pl.ANY)
    vmem = pl.BlockSpec(memory_space=pltpu.VMEM)
    shard, left_shard, *block = own.shape[1], own_left.shape[1], *own.shape[2:]
    return pl.pallas_call(
        select_kernel,
        out_shape=[jax.ShapeDtypeStruct((n, *block), own.dtype) for n in (shard, shard, 2 * left_shard)],
        in_specs=[pl.BlockSpec(memory_space=pltpu.SMEM), hbm, hbm],
        out_specs=[vmem] * 3,
        scratch_shapes=[pltpu.SemaphoreType.DMA((4,))],
        cost_estimate=pl.CostEstimate(flops=0, bytes_accessed=2**20, transcendentals=0),
        name="select_panels",
    )(core.reshape(1), own, own_left)


def products_kernel(stage, groups, entries, left, right, *refs):
    if stage == 0:
        start, acc = refs
        count = start.shape[0]
        acc[:count] = -3.0 * start[...].astype(jnp.float32)
        acc[count:] = jnp.zeros((acc.shape[0] - count, *acc.shape[1:]), jnp.float32)
    elif stage == 1:
        start, acc = refs[0], refs[-1]
        acc[...] = start[...]
    else:
        start, acc, out = refs[0], refs[-1], refs[-2]
        count = start.shape[0]
        at = 0
        for part in refs[1:-2]:
            size = part.shape[0]
            acc[at : at + size] = start[at : at + size] + part[...]
            at += size
        acc[count] = jnp.zeros_like(acc[count])

    def step(g, carry):
        words = [entries[stage, g * GROUP + e] for e in range(GROUP)]
        made = [
            jnp.dot(left[w & 255], right[(w >> 8) & 255], preferred_element_type=jnp.float32)
            for w in words
        ]
        for w, product in zip(words, made):
            slot = w >> 16
            acc[slot] = acc[slot] + product
        return carry

    lax.fori_loop(0, groups[stage], step, 0)
    if stage == 1:
        own = refs[1]
        at = own.shape[0]
        own[...] = acc[:at]
        for part in refs[2:-1]:
            part[...] = acc[at : at + part.shape[0]]
            at += part.shape[0]
    elif stage == 2:
        out[...] = (-0.5 * acc[:count]).astype(out.dtype)


def add_products(stage, groups, entries, left, right, starts, slots):
    smem = pl.BlockSpec(memory_space=pltpu.SMEM)
    vmem = pl.BlockSpec(memory_space=pltpu.VMEM)
    block = left.shape[-1]

    def result(count, dtype=jnp.float32):
        return jax.ShapeDtypeStruct((count, block, block), dtype)

    if stage == 0:
        outs, scratch = [result(2 * slots + 1)], []
    elif stage == 1:
        outs = [result(slots)] + [result(part) for part in PARTS]
        scratch = [pltpu.VMEM((2 * slots + 1, block, block), jnp.float32)]
    else:
        outs = [result(slots, jnp.bfloat16)]
        scratch = [pltpu.VMEM((slots + 1, block, block), jnp.float32)]
    return pl.pallas_call(
        functools.partial(products_kernel, stage),
        out_shape=outs,
        in_specs=[smem, smem] + [vmem] * (2 + len(starts)),
        out_specs=[vmem] * len(outs),
        scratch_shapes=scratch,
        cost_estimate=pl.CostEstimate(flops=2**20, bytes_accessed=2**20, transcendentals=0),
        compiler_params=pltpu.CompilerParams(vmem_limit_bytes=8 * 2**20),
        name="products",
    )(groups, entries, left, right, *starts)


def move(blocks, step):
    depth = lax.axis_size("col") // 2
    pairs = []
    for y in range(SIDE):
        for x in range(SIDE):
            for z in range(depth):
                for core in range(2):
                    tx, ty, tz, tcore = step(x, y, z, core)
                    to = ((ty % SIDE * SIDE + tx % SIDE) * depth + tz % depth) * 2 + tcore
                    pairs.append((((y * SIDE + x) * depth + z) * 2 + core, to))
    return lax.ppermute(blocks, ("row", "col"), pairs)


def sibling(blocks):
    return move(blocks, lambda x, y, z, c: (x, y, z, 1 - c))


def onward(blocks):
    return move(blocks, lambda x, y, z, c: (x, y, z + 1 - 2 * c, c))


def first(forth, back):
    return [
        move(v, lambda x, y, z, c: (x, y + by, z, c) if c else (x + by, y, z, c))
        for v, by in ((forth, 1), (back, -1))
    ]


def second(forth, back):
    return [
        move(v, lambda x, y, z, c: (x + by, y, z, c) if c else (x, y + by, z, c))
        for v, by in ((forth, 1), (back, -1))
    ]


def join(*pieces):
    return jnp.concatenate(pieces)


def on_device(x_panels, square_panels, x_blocks, pair_lists, pair_counts):
    block = x_blocks.shape[-1]
    left_shard, shard = x_panels.shape[2], square_panels.shape[2]
    pairs, slots = pair_lists.shape[-1], x_blocks.shape[1]
    depth = lax.axis_size("col") // 2
    row, col = lax.axis_index("row"), lax.axis_index("col")
    core = (col % 2).astype(jnp.int32)
    here = jnp.stack([row % SIDE, row // SIDE, col // 2, core]).astype(jnp.int32)
    order = lax.optimization_barrier
    scope = jax.named_scope

    own, own_left = square_panels[:, 0], x_panels[:, 0]
    keep, give, own_left = select_panels(core, own, own_left)
    with scope("w0"):
        got = sibling(give)
    with scope("w1"):
        got_left = sibling(own_left)
    lists = join(pair_lists.reshape(-1), pair_counts.reshape(-1))
    with scope("w2"):
        got_lists = sibling(lists)
    unit = join(keep, got)
    pair = join(own_left[:left_shard], got_left[left_shard:], own_left[left_shard:], got_left[:left_shard])

    unit, pair = order(unit), order(pair)
    with scope("s1"):
        r1, l1 = first(unit, unit)
    with scope("t"):
        t = second(unit, unit)
    entries, groups = sort_lists(here, lists, got_lists, left_shard, shard, depth, pairs, slots)
    half = 2 * left_shard
    with scope("z1"):
        z1 = onward(pair)
    with scope("z2"):
        z2 = onward(z1)
    with scope("z3"):
        z3 = onward(z2)
    with scope("z4"):
        z4 = onward(z3[:half])
    with scope("w4"):
        swapped = sibling(join(z1[half:], z2[half:], z3[half:]))
    left = join(pair[:half], z1[:half], z2[:half], z3[:half], z4, swapped)
    with scope("s2"):
        s2 = first(r1[:shard], l1[shard:])
    t, ar, al, entries, groups = order((t, r1, l1, entries, groups))
    with scope("a1"):
        a1 = second(ar, al)
    x2 = join(*s2)
    with scope("b"):
        b = second(x2, x2)
    with scope("ga"):
        ga = second(join(a1[0][shard:], l1[shard:]), join(a1[1][shard:], r1[shard:]))
    with scope("gh"):
        gh = second(join(t[0][:shard], b[0][:shard]), join(t[1][shard:], b[1][shard:]))
    near = join(unit, r1, l1, *s2, *t, *a1)
    (total,) = add_products(0, groups, entries, left, near, [x_blocks[0]], slots)
    ga, ar, al, a1 = order((ga, r1, l1, a1))
    with scope("a2"):
        a2 = second(join(a1[0][:shard], al[:shard]), join(a1[1][:shard], ar[:shard]))
    far = join(*b, *ga, *gh)
    total, *theirs = add_products(1, groups, entries, left, far, [total], slots)
    with scope("w3"):
        mine = [sibling(part) for part in theirs]
    return add_products(2, groups, entries, left, join(*a2), [total, *mine], slots)[0][None]


def solution(mesh):
    in_specs = (
        P(None, "row", "col", None, None),
        P(None, "row", "col", None, None),
        P("row", "col", None, None),
        P("row", "col", None, None, None),
        P("row", "col", None),
    )
    out_specs = P("row", "col", None, None)
    return jax.shard_map(
        on_device, mesh=mesh, in_specs=in_specs, out_specs=out_specs, check_vma=False
    )
```

```python
import functools

import jax
import jax.numpy as jnp
import numpy as np
from jax import lax
from jax.experimental import pallas as pl
from jax.experimental.pallas import tpu as pltpu
from jax.sharding import PartitionSpec as P

SIDE = 4
GROUP = 16
STAGES = 3
PARTS = (11, 11, 10)

UNITS = {
    (0, 0): ((0, 0), (0, 1)),
    (3, 0): ((0, 2), (0, 3)),
    (1, 0): ((0, 4), (0, 5)),
    (2, 0): ((0, 6), (0, 7)),
    (0, 3): ((0, 8), (0, 9)),
    (0, 1): ((0, 10), (0, 11)),
    (3, 3): ((0, 12), (0, 13)),
    (1, 1): ((0, 14), (0, 15)),
    (2, 3): ((1, 0), (1, 1)),
    (2, 1): ((1, 2), (1, 3)),
    (3, 2): ((2, 0), (1, 4)),
    (1, 3): ((2, 1), (1, 5)),
    (1, 2): ((2, 2), (1, 6)),
    (3, 1): ((2, 3), (1, 7)),
    (0, 2): ((1, 8), (1, 10)),
    (2, 2): ((1, 9), (1, 11)),
}


def place_right(shard):
    right = np.zeros((2, 2, SIDE, SIDE), np.int32)
    for core in range(2):
        for column in range(2):
            for dx in range(SIDE):
                for dy in range(SIDE):
                    stage, slot = UNITS[(dx, dy) if core == 0 else (dy, dx)][column]
                    right[core, column, dx, dy] = stage << 16 | slot * shard << 8
    return right.reshape(-1)


def sort_kernel(left_shard, shard, depth, pairs, slots, here, right_at, own, got, entries, groups, lengths, left_of, right_of):
    x, y, z, core = here[0], here[1], here[2], here[3]
    way = 2 * core - 1
    for stage in range(STAGES):
        lengths[stage] = 0

    def place(owner, carry):
        steps = (((owner >> 1) - z) * way) & (depth - 1)
        other = (owner & 1) ^ core
        far = depth + 2 + 2 * (depth - 1 - steps) + 1 - other
        at = jnp.where(steps <= depth // 2, 2 * steps + other, far)
        left_of[owner] = (at - owner) * left_shard
        dx = (owner - x) & (SIDE - 1)
        dy = ((owner >> 2) - y) & (SIDE - 1)
        for column in range(2):
            found = right_at[((core * 2 + column) * SIDE + dx) * SIDE + dy]
            right_of[column, owner] = found - (owner * shard << 8)
        return carry

    lax.fori_loop(0, SIDE * SIDE, place, 0)
    base = core * 3 * pairs
    for column, lists in enumerate((own, got)):

        def add(e, carry, column=column, lists=lists):
            first = lists[base + e]
            second = lists[base + pairs + e]
            slot = lists[base + 2 * pairs + e] + column * slots
            left = first + left_of[(first * (2**16 // left_shard + 1)) >> 16]
            found = right_of[column, (second * (2**16 // shard + 1)) >> 16] + (second << 8)
            stage = found >> 16
            at = lengths[stage]
            entries[stage, at] = left | (found & 0xFF00) | slot << 16
            lengths[stage] = at + 1
            return carry

        lax.fori_loop(0, lists[6 * pairs + core], add, 0)
    for stage in range(STAGES):
        length = lengths[stage]
        unused = (2 * slots if stage < 2 else slots) << 16
        for e in range(GROUP - 1):
            entries[stage, length + e] = unused
        groups[stage] = (length + GROUP - 1) // GROUP


def sort_lists(here, own, got, left_shard, shard, depth, pairs, slots):
    smem = pl.BlockSpec(memory_space=pltpu.SMEM)
    return pl.pallas_call(
        functools.partial(sort_kernel, left_shard, shard, depth, pairs, slots),
        out_shape=(
            jax.ShapeDtypeStruct((STAGES, 2 * pairs + GROUP), jnp.int32),
            jax.ShapeDtypeStruct((STAGES,), jnp.int32),
        ),
        in_specs=[smem] * 4,
        out_specs=(smem, smem),
        scratch_shapes=[
            pltpu.SMEM((STAGES,), jnp.int32),
            pltpu.SMEM((SIDE * SIDE,), jnp.int32),
            pltpu.SMEM((2, SIDE * SIDE), jnp.int32),
        ],
        cost_estimate=pl.CostEstimate(flops=0, bytes_accessed=8 * 2**20, transcendentals=0),
        name="sort_lists",
    )(here, jnp.asarray(place_right(shard)), own, got)


def select_kernel(core, own, own_left, keep, give, left, sems):
    c = core[0]
    size = own_left.shape[1]
    copies = [
        pltpu.make_async_copy(own.at[1 - c], give, sems.at[0]),
        pltpu.make_async_copy(own.at[c], keep, sems.at[1]),
        pltpu.make_async_copy(own_left.at[c], left.at[pl.ds(0, size)], sems.at[2]),
        pltpu.make_async_copy(own_left.at[1 - c], left.at[pl.ds(size, size)], sems.at[3]),
    ]
    for copy in copies:
        copy.start()
    for copy in copies:
        copy.wait()


def select_panels(core, own, own_left):
    hbm = pl.BlockSpec(memory_space=pl.ANY)
    vmem = pl.BlockSpec(memory_space=pltpu.VMEM)
    shard, left_shard, *block = own.shape[1], own_left.shape[1], *own.shape[2:]
    return pl.pallas_call(
        select_kernel,
        out_shape=[jax.ShapeDtypeStruct((n, *block), own.dtype) for n in (shard, shard, 2 * left_shard)],
        in_specs=[pl.BlockSpec(memory_space=pltpu.SMEM), hbm, hbm],
        out_specs=[vmem] * 3,
        scratch_shapes=[pltpu.SemaphoreType.DMA((4,))],
        cost_estimate=pl.CostEstimate(flops=0, bytes_accessed=2**20, transcendentals=0),
        name="select_panels",
    )(core.reshape(1), own, own_left)


def products_kernel(stage, groups, entries, left, right, *refs):
    if stage == 0:
        start, acc = refs
        count = start.shape[0]
        acc[:count] = -3.0 * start[...].astype(jnp.float32)
        acc[count:] = jnp.zeros((acc.shape[0] - count, *acc.shape[1:]), jnp.float32)
    elif stage == 1:
        start, acc = refs[0], refs[-1]
        acc[...] = start[...]
    else:
        start, acc, out = refs[0], refs[-1], refs[-2]
        count = start.shape[0]
        at = 0
        for part in refs[1:-2]:
            size = part.shape[0]
            acc[at : at + size] = start[at : at + size] + part[...]
            at += size
        acc[count] = jnp.zeros_like(acc[count])

    def step(g, carry):
        words = [entries[stage, g * GROUP + e] for e in range(GROUP)]
        made = [
            jnp.dot(left[w & 255], right[(w >> 8) & 255], preferred_element_type=jnp.float32)
            for w in words
        ]
        for w, product in zip(words, made):
            slot = w >> 16
            acc[slot] = acc[slot] + product
        return carry

    lax.fori_loop(0, groups[stage], step, 0)
    if stage == 1:
        own = refs[1]
        at = own.shape[0]
        own[...] = acc[:at]
        for part in refs[2:-1]:
            part[...] = acc[at : at + part.shape[0]]
            at += part.shape[0]
    elif stage == 2:
        out[...] = (-0.5 * acc[:count]).astype(out.dtype)


def add_products(stage, groups, entries, left, right, starts, slots):
    smem = pl.BlockSpec(memory_space=pltpu.SMEM)
    vmem = pl.BlockSpec(memory_space=pltpu.VMEM)
    block = left.shape[-1]

    def result(count, dtype=jnp.float32):
        return jax.ShapeDtypeStruct((count, block, block), dtype)

    if stage == 0:
        outs, scratch = [result(2 * slots + 1)], []
    elif stage == 1:
        outs = [result(slots)] + [result(part) for part in PARTS]
        scratch = [pltpu.VMEM((2 * slots + 1, block, block), jnp.float32)]
    else:
        outs = [result(slots, jnp.bfloat16)]
        scratch = [pltpu.VMEM((slots + 1, block, block), jnp.float32)]
    return pl.pallas_call(
        functools.partial(products_kernel, stage),
        out_shape=outs,
        in_specs=[smem, smem] + [vmem] * (2 + len(starts)),
        out_specs=[vmem] * len(outs),
        scratch_shapes=scratch,
        cost_estimate=pl.CostEstimate(flops=2**20, bytes_accessed=2**20, transcendentals=0),
        compiler_params=pltpu.CompilerParams(vmem_limit_bytes=8 * 2**20),
        name="products",
    )(groups, entries, left, right, *starts)


def move(blocks, step):
    depth = lax.axis_size("col") // 2
    pairs = []
    for y in range(SIDE):
        for x in range(SIDE):
            for z in range(depth):
                for core in range(2):
                    tx, ty, tz, tcore = step(x, y, z, core)
                    to = ((ty % SIDE * SIDE + tx % SIDE) * depth + tz % depth) * 2 + tcore
                    pairs.append((((y * SIDE + x) * depth + z) * 2 + core, to))
    return lax.ppermute(blocks, ("row", "col"), pairs)


def sibling(blocks):
    return move(blocks, lambda x, y, z, c: (x, y, z, 1 - c))


def onward(blocks):
    return move(blocks, lambda x, y, z, c: (x, y, z + 1 - 2 * c, c))


def first(forth, back):
    return [
        move(v, lambda x, y, z, c: (x, y + by, z, c) if c else (x + by, y, z, c))
        for v, by in ((forth, 1), (back, -1))
    ]


def second(forth, back):
    return [
        move(v, lambda x, y, z, c: (x + by, y, z, c) if c else (x, y + by, z, c))
        for v, by in ((forth, 1), (back, -1))
    ]


def join(*pieces):
    return jnp.concatenate(pieces)


def on_device(x_panels, square_panels, x_blocks, pair_lists, pair_counts):
    block = x_blocks.shape[-1]
    left_shard, shard = x_panels.shape[2], square_panels.shape[2]
    pairs, slots = pair_lists.shape[-1], x_blocks.shape[1]
    depth = lax.axis_size("col") // 2
    row, col = lax.axis_index("row"), lax.axis_index("col")
    core = (col % 2).astype(jnp.int32)
    here = jnp.stack([row % SIDE, row // SIDE, col // 2, core]).astype(jnp.int32)
    order = lax.optimization_barrier
    scope = jax.named_scope

    own, own_left = square_panels[:, 0], x_panels[:, 0]
    keep, give, own_left = select_panels(core, own, own_left)
    with scope("w0"):
        got = sibling(give)
    with scope("w1"):
        got_left = sibling(own_left)
    lists = join(pair_lists.reshape(-1), pair_counts.reshape(-1))
    with scope("w2"):
        got_lists = sibling(lists)
    unit = join(keep, got)
    pair = join(own_left[:left_shard], got_left[left_shard:], own_left[left_shard:], got_left[:left_shard])

    unit, pair = order(unit), order(pair)
    with scope("s1"):
        r1, l1 = first(unit, unit)
    with scope("t"):
        t = second(unit, unit)
    entries, groups = sort_lists(here, lists, got_lists, left_shard, shard, depth, pairs, slots)
    half = 2 * left_shard
    with scope("z1"):
        z1 = onward(pair)
    with scope("z2"):
        z2 = onward(z1)
    with scope("z3"):
        z3 = onward(z2)
    with scope("z4"):
        z4 = onward(z3[:half])
    with scope("w4"):
        swapped = sibling(join(z1[half:], z2[half:], z3[half:]))
    left = join(pair[:half], z1[:half], z2[:half], z3[:half], z4, swapped)
    near1, z1 = order(((r1, l1), z1))
    with scope("s2"):
        s2 = first(near1[0][:shard], near1[1][shard:])
    t, ar, al, entries, groups = order((t, r1, l1, entries, groups))
    with scope("a1"):
        a1 = second(ar, al)
    x2 = join(*s2)
    with scope("b"):
        b = second(x2, x2)
    with scope("ga"):
        ga = second(join(a1[0][shard:], l1[shard:]), join(a1[1][shard:], r1[shard:]))
    with scope("gh"):
        gh = second(join(t[0][:shard], b[0][:shard]), join(t[1][shard:], b[1][shard:]))
    near = join(unit, r1, l1, *s2, *t, *a1)
    (total,) = add_products(0, groups, entries, left, near, [x_blocks[0]], slots)
    ga, ar, al, a1 = order((ga, r1, l1, a1))
    with scope("a2"):
        a2 = second(join(a1[0][:shard], al[:shard]), join(a1[1][:shard], ar[:shard]))
    far = join(*b, *ga, *gh)
    total, *theirs = add_products(1, groups, entries, left, far, [total], slots)
    with scope("w3"):
        mine = [sibling(part) for part in theirs]
    return add_products(2, groups, entries, left, join(*a2), [total, *mine], slots)[0][None]


def solution(mesh):
    in_specs = (
        P(None, "row", "col", None, None),
        P(None, "row", "col", None, None),
        P("row", "col", None, None),
        P("row", "col", None, None, None),
        P("row", "col", None),
    )
    out_specs = P("row", "col", None, None)
    return jax.shard_map(
        on_device, mesh=mesh, in_specs=in_specs, out_specs=out_specs, check_vma=False
    )
```

```python
import functools

import jax
import jax.numpy as jnp
import numpy as np
from jax import lax
from jax.experimental import pallas as pl
from jax.experimental.pallas import tpu as pltpu
from jax.sharding import PartitionSpec as P

SIDE = 4
GROUP = 16
STAGES = 3
PARTS = (11, 11, 10)

UNITS = {
    (0, 0): ((0, 0), (0, 1)),
    (3, 0): ((0, 2), (0, 3)),
    (1, 0): ((0, 4), (0, 5)),
    (2, 0): ((0, 6), (0, 7)),
    (0, 3): ((0, 8), (0, 9)),
    (0, 1): ((0, 10), (0, 11)),
    (3, 3): ((0, 12), (0, 13)),
    (1, 1): ((0, 14), (0, 15)),
    (2, 3): ((1, 0), (1, 1)),
    (2, 1): ((1, 2), (1, 3)),
    (3, 2): ((2, 0), (1, 4)),
    (1, 3): ((2, 1), (1, 5)),
    (1, 2): ((2, 2), (1, 6)),
    (3, 1): ((2, 3), (1, 7)),
    (0, 2): ((1, 8), (1, 10)),
    (2, 2): ((1, 9), (1, 11)),
}


def place_right(shard):
    right = np.zeros((2, 2, SIDE, SIDE), np.int32)
    for core in range(2):
        for column in range(2):
            for dx in range(SIDE):
                for dy in range(SIDE):
                    stage, slot = UNITS[(dx, dy) if core == 0 else (dy, dx)][column]
                    right[core, column, dx, dy] = stage << 16 | slot * shard << 8
    return right.reshape(-1)


def sort_kernel(left_shard, shard, depth, pairs, slots, here, right_at, own, got, entries, groups, lengths, left_of, right_of):
    x, y, z, core = here[0], here[1], here[2], here[3]
    way = 2 * core - 1
    for stage in range(STAGES):
        lengths[stage] = 0

    def place(owner, carry):
        steps = (((owner >> 1) - z) * way) & (depth - 1)
        other = (owner & 1) ^ core
        far = depth + 2 + 2 * (depth - 1 - steps) + 1 - other
        at = jnp.where(steps <= depth // 2, 2 * steps + other, far)
        left_of[owner] = (at - owner) * left_shard
        dx = (owner - x) & (SIDE - 1)
        dy = ((owner >> 2) - y) & (SIDE - 1)
        for column in range(2):
            found = right_at[((core * 2 + column) * SIDE + dx) * SIDE + dy]
            right_of[column, owner] = found - (owner * shard << 8)
        return carry

    lax.fori_loop(0, SIDE * SIDE, place, 0)
    base = core * 3 * pairs
    for column, lists in enumerate((own, got)):

        def add(e, carry, column=column, lists=lists):
            first = lists[base + e]
            second = lists[base + pairs + e]
            slot = lists[base + 2 * pairs + e] + column * slots
            left = first + left_of[(first * (2**16 // left_shard + 1)) >> 16]
            found = right_of[column, (second * (2**16 // shard + 1)) >> 16] + (second << 8)
            stage = found >> 16
            at = lengths[stage]
            entries[stage, at] = left | (found & 0xFF00) | slot << 16
            lengths[stage] = at + 1
            return carry

        lax.fori_loop(0, lists[6 * pairs + core], add, 0)
    for stage in range(STAGES):
        length = lengths[stage]
        unused = (2 * slots if stage < 2 else slots) << 16
        for e in range(GROUP - 1):
            entries[stage, length + e] = unused
        groups[stage] = (length + GROUP - 1) // GROUP


def sort_lists(here, own, got, left_shard, shard, depth, pairs, slots):
    smem = pl.BlockSpec(memory_space=pltpu.SMEM)
    return pl.pallas_call(
        functools.partial(sort_kernel, left_shard, shard, depth, pairs, slots),
        out_shape=(
            jax.ShapeDtypeStruct((STAGES, 2 * pairs + GROUP), jnp.int32),
            jax.ShapeDtypeStruct((STAGES,), jnp.int32),
        ),
        in_specs=[smem] * 4,
        out_specs=(smem, smem),
        scratch_shapes=[
            pltpu.SMEM((STAGES,), jnp.int32),
            pltpu.SMEM((SIDE * SIDE,), jnp.int32),
            pltpu.SMEM((2, SIDE * SIDE), jnp.int32),
        ],
        cost_estimate=pl.CostEstimate(flops=0, bytes_accessed=8 * 2**20, transcendentals=0),
        name="sort_lists",
    )(here, jnp.asarray(place_right(shard)), own, got)


def products_kernel(stage, groups, entries, left, right, *refs):
    if stage == 0:
        start, acc = refs
        count = start.shape[0]
        acc[:count] = -3.0 * start[...].astype(jnp.float32)
        acc[count:] = jnp.zeros((acc.shape[0] - count, *acc.shape[1:]), jnp.float32)
    elif stage == 1:
        start, acc = refs[0], refs[-1]
        acc[...] = start[...]
    else:
        start, acc, out = refs[0], refs[-1], refs[-2]
        count = start.shape[0]
        at = 0
        for part in refs[1:-2]:
            size = part.shape[0]
            acc[at : at + size] = start[at : at + size] + part[...]
            at += size
        acc[count] = jnp.zeros_like(acc[count])

    def step(g, carry):
        words = [entries[stage, g * GROUP + e] for e in range(GROUP)]
        made = [
            jnp.dot(left[w & 255], right[(w >> 8) & 255], preferred_element_type=jnp.float32)
            for w in words
        ]
        for w, product in zip(words, made):
            slot = w >> 16
            acc[slot] = acc[slot] + product
        return carry

    lax.fori_loop(0, groups[stage], step, 0)
    if stage == 1:
        own = refs[1]
        at = own.shape[0]
        own[...] = acc[:at]
        for part in refs[2:-1]:
            part[...] = acc[at : at + part.shape[0]]
            at += part.shape[0]
    elif stage == 2:
        out[...] = (-0.5 * acc[:count]).astype(out.dtype)


def add_products(stage, groups, entries, left, right, starts, slots):
    smem = pl.BlockSpec(memory_space=pltpu.SMEM)
    vmem = pl.BlockSpec(memory_space=pltpu.VMEM)
    block = left.shape[-1]

    def result(count, dtype=jnp.float32):
        return jax.ShapeDtypeStruct((count, block, block), dtype)

    if stage == 0:
        outs, scratch = [result(2 * slots + 1)], []
    elif stage == 1:
        outs = [result(slots)] + [result(part) for part in PARTS]
        scratch = [pltpu.VMEM((2 * slots + 1, block, block), jnp.float32)]
    else:
        outs = [result(slots, jnp.bfloat16)]
        scratch = [pltpu.VMEM((slots + 1, block, block), jnp.float32)]
    return pl.pallas_call(
        functools.partial(products_kernel, stage),
        out_shape=outs,
        in_specs=[smem, smem] + [vmem] * (2 + len(starts)),
        out_specs=[vmem] * len(outs),
        scratch_shapes=scratch,
        cost_estimate=pl.CostEstimate(flops=2**20, bytes_accessed=2**20, transcendentals=0),
        compiler_params=pltpu.CompilerParams(vmem_limit_bytes=8 * 2**20),
        name="products",
    )(groups, entries, left, right, *starts)


def move(blocks, step):
    depth = lax.axis_size("col") // 2
    pairs = []
    for y in range(SIDE):
        for x in range(SIDE):
            for z in range(depth):
                for core in range(2):
                    tx, ty, tz, tcore = step(x, y, z, core)
                    to = ((ty % SIDE * SIDE + tx % SIDE) * depth + tz % depth) * 2 + tcore
                    pairs.append((((y * SIDE + x) * depth + z) * 2 + core, to))
    return lax.ppermute(blocks, ("row", "col"), pairs)


def sibling(blocks):
    return move(blocks, lambda x, y, z, c: (x, y, z, 1 - c))


def onward(blocks):
    return move(blocks, lambda x, y, z, c: (x, y, z + 1 - 2 * c, c))


def first(forth, back):
    return [
        move(v, lambda x, y, z, c: (x, y + by, z, c) if c else (x + by, y, z, c))
        for v, by in ((forth, 1), (back, -1))
    ]


def second(forth, back):
    return [
        move(v, lambda x, y, z, c: (x + by, y, z, c) if c else (x, y + by, z, c))
        for v, by in ((forth, 1), (back, -1))
    ]


def join(*pieces):
    return jnp.concatenate(pieces)


def on_device(x_panels, square_panels, x_blocks, pair_lists, pair_counts):
    block = x_blocks.shape[-1]
    left_shard, shard = x_panels.shape[2], square_panels.shape[2]
    pairs, slots = pair_lists.shape[-1], x_blocks.shape[1]
    depth = lax.axis_size("col") // 2
    row, col = lax.axis_index("row"), lax.axis_index("col")
    core = (col % 2).astype(jnp.int32)
    here = jnp.stack([row % SIDE, row // SIDE, col // 2, core]).astype(jnp.int32)
    order = lax.optimization_barrier
    scope = jax.named_scope

    own, own_left = square_panels[:, 0], x_panels[:, 0]
    with scope("w0"):
        got = sibling(own)
    with scope("w1"):
        got_left = sibling(own_left)
    lists = join(pair_lists.reshape(-1), pair_counts.reshape(-1))
    with scope("w2"):
        got_lists = sibling(lists)

    def panel(blocks, other=False):
        return jnp.where((core == 1) != other, blocks[1], blocks[0])

    unit = join(panel(own), panel(got))
    pair = join(panel(own_left), panel(got_left), panel(own_left, True), panel(got_left, True))

    unit, pair = order((unit, pair))
    with scope("s1"):
        r1, l1 = first(unit, unit)
    with scope("t"):
        t = second(unit, unit)
    entries, groups = sort_lists(here, lists, got_lists, left_shard, shard, depth, pairs, slots)
    half = 2 * left_shard
    with scope("z1"):
        z1 = onward(pair)
    with scope("z2"):
        z2 = onward(z1)
    with scope("z3"):
        z3 = onward(z2)
    with scope("z4"):
        z4 = onward(z3[:half])
    with scope("w4"):
        swapped = sibling(join(z1[half:], z2[half:], z3[half:]))
    left = join(pair[:half], z1[:half], z2[:half], z3[:half], z4, swapped)
    near1 = r1, l1
    with scope("s2"):
        s2 = first(near1[0][:shard], near1[1][shard:])
    t, ar, al, entries, groups = order((t, r1, l1, entries, groups))
    with scope("a1"):
        a1 = second(ar, al)
    x2 = join(*s2)
    with scope("b"):
        b = second(x2, x2)
    with scope("ga"):
        ga = second(join(a1[0][shard:], l1[shard:]), join(a1[1][shard:], r1[shard:]))
    with scope("gh"):
        gh = second(join(t[0][:shard], b[0][:shard]), join(t[1][shard:], b[1][shard:]))
    near = join(unit, r1, l1, *s2, *t, *a1)
    (total,) = add_products(0, groups, entries, left, near, [x_blocks[0]], slots)
    ga, ar, al, a1 = order((ga, r1, l1, a1))
    with scope("a2"):
        a2 = second(join(a1[0][:shard], al[:shard]), join(a1[1][:shard], ar[:shard]))
    far = join(*b, *ga, *gh)
    total, *theirs = add_products(1, groups, entries, left, far, [total], slots)
    with scope("w3"):
        mine = [sibling(part) for part in theirs]
    return add_products(2, groups, entries, left, join(*a2), [total, *mine], slots)[0][None]


def solution(mesh):
    in_specs = (
        P(None, "row", "col", None, None),
        P(None, "row", "col", None, None),
        P("row", "col", None, None),
        P("row", "col", None, None, None),
        P("row", "col", None),
    )
    out_specs = P("row", "col", None, None)
    return jax.shard_map(
        on_device, mesh=mesh, in_specs=in_specs, out_specs=out_specs, check_vma=False
    )
```

```python
import functools

import jax
import jax.numpy as jnp
import numpy as np
from jax import lax
from jax.experimental import pallas as pl
from jax.experimental.pallas import tpu as pltpu
from jax.sharding import PartitionSpec as P

SIDE = 4
GROUP = 32
STAGES = 3
PARTS = (11, 11, 10)

UNITS = {
    (0, 0): ((0, 0), (0, 1)),
    (3, 0): ((0, 2), (0, 3)),
    (1, 0): ((0, 4), (0, 5)),
    (2, 0): ((0, 6), (0, 7)),
    (0, 3): ((0, 8), (0, 9)),
    (0, 1): ((0, 10), (0, 11)),
    (3, 3): ((0, 12), (0, 13)),
    (1, 1): ((0, 14), (0, 15)),
    (2, 3): ((1, 0), (1, 1)),
    (2, 1): ((1, 2), (1, 3)),
    (3, 2): ((2, 0), (1, 4)),
    (1, 3): ((2, 1), (1, 5)),
    (1, 2): ((2, 2), (1, 6)),
    (3, 1): ((2, 3), (1, 7)),
    (0, 2): ((1, 8), (1, 10)),
    (2, 2): ((1, 9), (1, 11)),
}


def place_right(shard):
    right = np.zeros((2, 2, SIDE, SIDE), np.int32)
    for core in range(2):
        for column in range(2):
            for dx in range(SIDE):
                for dy in range(SIDE):
                    stage, slot = UNITS[(dx, dy) if core == 0 else (dy, dx)][column]
                    right[core, column, dx, dy] = stage << 16 | slot * shard << 8
    return right.reshape(-1)


def sort_kernel(left_shard, shard, depth, pairs, slots, here, right_at, own, got, entries, groups, lengths, left_of, right_of):
    x, y, z, core = here[0], here[1], here[2], here[3]
    way = 2 * core - 1
    for stage in range(STAGES):
        lengths[stage] = 0

    def place(owner, carry):
        steps = (((owner >> 1) - z) * way) & (depth - 1)
        other = (owner & 1) ^ core
        far = depth + 2 + 2 * (depth - 1 - steps) + 1 - other
        at = jnp.where(steps <= depth // 2, 2 * steps + other, far)
        left_of[owner] = (at - owner) * left_shard
        dx = (owner - x) & (SIDE - 1)
        dy = ((owner >> 2) - y) & (SIDE - 1)
        for column in range(2):
            found = right_at[((core * 2 + column) * SIDE + dx) * SIDE + dy]
            right_of[column, owner] = found - (owner * shard << 8)
        return carry

    lax.fori_loop(0, SIDE * SIDE, place, 0)
    base = core * 3 * pairs
    for column, lists in enumerate((own, got)):

        def add(e, carry, column=column, lists=lists):
            first = lists[base + e]
            second = lists[base + pairs + e]
            slot = lists[base + 2 * pairs + e] + column * slots
            left = first + left_of[(first * (2**16 // left_shard + 1)) >> 16]
            found = right_of[column, (second * (2**16 // shard + 1)) >> 16] + (second << 8)
            stage = found >> 16
            at = lengths[stage]
            entries[stage, at] = left | (found & 0xFF00) | slot << 16
            lengths[stage] = at + 1
            return carry

        lax.fori_loop(0, lists[6 * pairs + core], add, 0)
    for stage in range(STAGES):
        length = lengths[stage]
        unused = (2 * slots if stage < 2 else slots) << 16
        for e in range(GROUP - 1):
            entries[stage, length + e] = unused
        groups[stage] = (length + GROUP - 1) // GROUP


def sort_lists(here, own, got, left_shard, shard, depth, pairs, slots):
    smem = pl.BlockSpec(memory_space=pltpu.SMEM)
    return pl.pallas_call(
        functools.partial(sort_kernel, left_shard, shard, depth, pairs, slots),
        out_shape=(
            jax.ShapeDtypeStruct((STAGES, 2 * pairs + GROUP), jnp.int32),
            jax.ShapeDtypeStruct((STAGES,), jnp.int32),
        ),
        in_specs=[smem] * 4,
        out_specs=(smem, smem),
        scratch_shapes=[
            pltpu.SMEM((STAGES,), jnp.int32),
            pltpu.SMEM((SIDE * SIDE,), jnp.int32),
            pltpu.SMEM((2, SIDE * SIDE), jnp.int32),
        ],
        cost_estimate=pl.CostEstimate(flops=0, bytes_accessed=8 * 2**20, transcendentals=0),
        name="sort_lists",
    )(here, jnp.asarray(place_right(shard)), own, got)


def products_kernel(stage, groups, entries, left, right, *refs):
    if stage == 0:
        start, acc = refs
        count = start.shape[0]
        acc[:count] = -3.0 * start[...].astype(jnp.float32)
        acc[count:] = jnp.zeros((acc.shape[0] - count, *acc.shape[1:]), jnp.float32)
    elif stage == 1:
        start, acc = refs[0], refs[-1]
        acc[...] = start[...]
    else:
        start, acc, out = refs[0], refs[-1], refs[-2]
        count = start.shape[0]
        at = 0
        for part in refs[1:-2]:
            size = part.shape[0]
            acc[at : at + size] = start[at : at + size] + part[...]
            at += size
        acc[count] = jnp.zeros_like(acc[count])

    def step(g, carry):
        words = [entries[stage, g * GROUP + e] for e in range(GROUP)]
        made = [
            jnp.dot(left[w & 255], right[(w >> 8) & 255], preferred_element_type=jnp.float32)
            for w in words
        ]
        for w, product in zip(words, made):
            slot = w >> 16
            acc[slot] = acc[slot] + product
        return carry

    lax.fori_loop(0, groups[stage], step, 0)
    if stage == 1:
        own = refs[1]
        at = own.shape[0]
        own[...] = acc[:at]
        for part in refs[2:-1]:
            part[...] = acc[at : at + part.shape[0]]
            at += part.shape[0]
    elif stage == 2:
        out[...] = (-0.5 * acc[:count]).astype(out.dtype)


def add_products(stage, groups, entries, left, right, starts, slots):
    smem = pl.BlockSpec(memory_space=pltpu.SMEM)
    vmem = pl.BlockSpec(memory_space=pltpu.VMEM)
    block = left.shape[-1]

    def result(count, dtype=jnp.float32):
        return jax.ShapeDtypeStruct((count, block, block), dtype)

    if stage == 0:
        outs, scratch = [result(2 * slots + 1)], []
    elif stage == 1:
        outs = [result(slots)] + [result(part) for part in PARTS]
        scratch = [pltpu.VMEM((2 * slots + 1, block, block), jnp.float32)]
    else:
        outs = [result(slots, jnp.bfloat16)]
        scratch = [pltpu.VMEM((slots + 1, block, block), jnp.float32)]
    return pl.pallas_call(
        functools.partial(products_kernel, stage),
        out_shape=outs,
        in_specs=[smem, smem] + [vmem] * (2 + len(starts)),
        out_specs=[vmem] * len(outs),
        scratch_shapes=scratch,
        cost_estimate=pl.CostEstimate(flops=2**20, bytes_accessed=2**20, transcendentals=0),
        compiler_params=pltpu.CompilerParams(vmem_limit_bytes=8 * 2**20),
        name="products",
    )(groups, entries, left, right, *starts)


def move(blocks, step):
    depth = lax.axis_size("col") // 2
    pairs = []
    for y in range(SIDE):
        for x in range(SIDE):
            for z in range(depth):
                for core in range(2):
                    tx, ty, tz, tcore = step(x, y, z, core)
                    to = ((ty % SIDE * SIDE + tx % SIDE) * depth + tz % depth) * 2 + tcore
                    pairs.append((((y * SIDE + x) * depth + z) * 2 + core, to))
    return lax.ppermute(blocks, ("row", "col"), pairs)


def sibling(blocks):
    return move(blocks, lambda x, y, z, c: (x, y, z, 1 - c))


def onward(blocks):
    return move(blocks, lambda x, y, z, c: (x, y, z + 1 - 2 * c, c))


def first(forth, back):
    return [
        move(v, lambda x, y, z, c: (x, y + by, z, c) if c else (x + by, y, z, c))
        for v, by in ((forth, 1), (back, -1))
    ]


def second(forth, back):
    return [
        move(v, lambda x, y, z, c: (x + by, y, z, c) if c else (x, y + by, z, c))
        for v, by in ((forth, 1), (back, -1))
    ]


def join(*pieces):
    return jnp.concatenate(pieces)


def on_device(x_panels, square_panels, x_blocks, pair_lists, pair_counts):
    block = x_blocks.shape[-1]
    left_shard, shard = x_panels.shape[2], square_panels.shape[2]
    pairs, slots = pair_lists.shape[-1], x_blocks.shape[1]
    depth = lax.axis_size("col") // 2
    row, col = lax.axis_index("row"), lax.axis_index("col")
    core = (col % 2).astype(jnp.int32)
    here = jnp.stack([row % SIDE, row // SIDE, col // 2, core]).astype(jnp.int32)
    order = lax.optimization_barrier
    scope = jax.named_scope

    own, own_left = square_panels[:, 0], x_panels[:, 0]
    with scope("w0"):
        got = sibling(own)
    with scope("w1"):
        got_left = sibling(own_left)
    lists = join(pair_lists.reshape(-1), pair_counts.reshape(-1))
    with scope("w2"):
        got_lists = sibling(lists)

    def panel(blocks, other=False):
        return jnp.where((core == 1) != other, blocks[1], blocks[0])

    unit = join(panel(own), panel(got))
    pair = join(panel(own_left), panel(got_left), panel(own_left, True), panel(got_left, True))

    unit, pair = order((unit, pair))
    with scope("s1"):
        r1, l1 = first(unit, unit)
    with scope("t"):
        t = second(unit, unit)
    entries, groups = sort_lists(here, lists, got_lists, left_shard, shard, depth, pairs, slots)
    half = 2 * left_shard
    with scope("z1"):
        z1 = onward(pair)
    with scope("z2"):
        z2 = onward(z1)
    with scope("z3"):
        z3 = onward(z2)
    with scope("z4"):
        z4 = onward(z3[:half])
    with scope("w4"):
        swapped = sibling(join(z1[half:], z2[half:], z3[half:]))
    left = join(pair[:half], z1[:half], z2[:half], z3[:half], z4, swapped)
    near1 = r1, l1
    with scope("s2"):
        s2 = first(near1[0][:shard], near1[1][shard:])
    t, ar, al, entries, groups = order((t, r1, l1, entries, groups))
    with scope("a1"):
        a1 = second(ar, al)
    x2 = join(*s2)
    with scope("b"):
        b = second(x2, x2)
    with scope("ga"):
        ga = second(join(a1[0][shard:], l1[shard:]), join(a1[1][shard:], r1[shard:]))
    with scope("gh"):
        gh = second(join(t[0][:shard], b[0][:shard]), join(t[1][shard:], b[1][shard:]))
    near = join(unit, r1, l1, *s2, *t, *a1)
    (total,) = add_products(0, groups, entries, left, near, [x_blocks[0]], slots)
    ga, ar, al, a1 = order((ga, r1, l1, a1))
    with scope("a2"):
        a2 = second(join(a1[0][:shard], al[:shard]), join(a1[1][:shard], ar[:shard]))
    far = join(*b, *ga, *gh)
    total, *theirs = add_products(1, groups, entries, left, far, [total], slots)
    with scope("w3"):
        mine = [sibling(part) for part in theirs]
    return add_products(2, groups, entries, left, join(*a2), [total, *mine], slots)[0][None]


def solution(mesh):
    in_specs = (
        P(None, "row", "col", None, None),
        P(None, "row", "col", None, None),
        P("row", "col", None, None),
        P("row", "col", None, None, None),
        P("row", "col", None),
    )
    out_specs = P("row", "col", None, None)
    return jax.shard_map(
        on_device, mesh=mesh, in_specs=in_specs, out_specs=out_specs, check_vma=False
    )
```
